32 devices in a mesh: groups: 2 (over y), dp: 8 (over z, x), tensor: 2 (over core).
Axes of the slice: x: 2, y: 2, z: 4, core: 2. Of those that a mesh axis runs over, the one named last changes fastest.
Arguments:
- queries: bfloat16 [4096, 4096], P(('groups', 'dp'), 'tensor'), parts along dimension 0
- keys: bfloat16 [4096, 512], P(('groups', 'dp'), 'tensor'), parts along dimension 0
- values: bfloat16 [4096, 512], P(('groups', 'dp'), 'tensor'), parts along dimension 0, may hold values from -6 to 6
- segments: int32 [4096], P(('groups', 'dp')), parts along dimension 0, may hold values from 0 to 255, as said below
- partner: int32 [16], P('groups'), parts along dimension 0, may hold values from 0 to 7, as said below
Outputs:
- near: bfloat16 [4096, 2048], P(('groups', 'dp'), 'tensor'), parts along dimension 0
- lent: bfloat16 [4096, 2048], P(('groups', 'dp'), 'tensor'), parts along dimension 0
The draws below stay inside these ranges and needn't reach their ends.
There are 2 independent parts, one for each index of `groups`. The reference program is written for one: setup_inputs(seed, part) draws one part's arguments, and reference() takes and returns one part's arrays. A program takes and returns all parts, laid end to end along the dimension named above; each array names one. Nothing has to cross between parts.
Inputs may be any that keep to these rules, and one draw needn't show every extreme that they name: `segments`: within each micro-batch the ids start at 0 and rise by 0 or 1 from one token to the next; in some micro-batch they reach 255. partner[partner[b]] == b and partner[b] != b for every b.
All inputs are finite; a program needn't handle non-finite values.
Results may differ from the reference program's by a relative error of at most 0.0023.
Values may be sent and summed in bfloat16 or wider, within the bound.
No kernel may reach another device: no remote copies, remote signals or barrier semaphores. Data moves between devices by JAX's collectives and lax.ppermute only.
A program may use at most 64 MiB of HBM per device.

```python
import jax
import jax.numpy as jnp
from jax import lax

QUERY_HEADS = 32
KEY_VALUE_HEADS = 4
HEAD_SIZE = 128
TOK_DEV = 256
GROUP_TOKENS = 2048
N_DP = 8


def base_keys(key):
    return jax.random.normal(key, (GROUP_TOKENS, KEY_VALUE_HEADS * HEAD_SIZE), jnp.float32)


def rank_exponents(key):
    inner = jax.random.fold_in(key, 21)
    first_key, second_key = jax.random.split(inner, 2)
    exponent = jax.random.randint(first_key, (N_DP,), 2, 10)
    chosen = jax.random.randint(second_key, (), 0, N_DP)
    return jnp.where(jnp.arange(N_DP) == chosen, 0, exponent).astype(jnp.int32)


def draw_keys(key, part):
    base = base_keys(key)
    return base.astype(jnp.bfloat16)


def draw_queries(key, part):
    key = jax.random.fold_in(key, 5)
    fresh = jax.random.normal(key, (GROUP_TOKENS, QUERY_HEADS * HEAD_SIZE), jnp.float32)
    return fresh.astype(jnp.bfloat16)


def draw_segments(key, part):
    exponent = rank_exponents(key)[:, None]
    key = jax.random.fold_in(key, 11)
    micro_batch_rows = TOK_DEV
    raw_bits = jax.random.randint(key, (N_DP, micro_batch_rows), 0, 1 << 20)
    starts = raw_bits % 2 ** exponent == 0
    starts = starts & (jnp.arange(micro_batch_rows)[None, :] > 0)
    ids = jnp.cumsum(starts.astype(jnp.int32), axis=1)
    return ids.reshape(N_DP * micro_batch_rows).astype(jnp.int32)


def draw_partner(key, part):
    exponent = rank_exponents(key)
    score = exponent * N_DP + jnp.arange(N_DP, dtype=jnp.int32)
    order = jnp.argsort(score, stable=True).astype(jnp.int32)
    matched = jnp.zeros((N_DP,), jnp.int32).at[order].set(order[::-1])
    return matched.astype(jnp.int32)


def block_scale(stream_key, shape, pieces, least, largest):
    loudness, own = 1.0, jax.random.fold_in(stream_key, 6)
    for axis_at, shards_of in pieces:
        draws = jnp.exp(jax.random.uniform(jax.random.fold_in(own, axis_at), (shards_of,), jnp.float32, least / len(pieces), largest / len(pieces)))
        loudness = loudness * jnp.repeat(draws, shape[axis_at] // shards_of).reshape([-1 if axis == axis_at else 1 for axis in range(len(shape))])
    return loudness


def centred(own_key, extent, deviation, bound, pieces=(), held_as=jnp.bfloat16):
    gain = block_scale(own_key, extent, pieces, -0.22, 0.18) if pieces else 1.0
    array = jax.random.normal(own_key, extent, jnp.float32) * deviation * gain
    return jnp.minimum(jnp.maximum(array, -bound), bound).astype(held_as)


def setup_inputs(seed: int = 0, part: int = 0) -> dict:
    splits = jax.random.split(jax.random.key(seed), 6)
    own_keys = jax.random.split(jax.random.fold_in(splits[5], part), 6)
    queries = draw_queries(jax.random.fold_in(jax.random.fold_in(splits[5], part), 71), part)
    keys = draw_keys(jax.random.fold_in(jax.random.fold_in(splits[5], part), 71), part)
    values = centred(own_keys[2], (GROUP_TOKENS, KEY_VALUE_HEADS * HEAD_SIZE), 1.0, 6.0, ((0, 8), (1, 2)))
    segments = draw_segments(jax.random.fold_in(jax.random.fold_in(splits[5], part), 71), part)
    partner = draw_partner(jax.random.fold_in(jax.random.fold_in(splits[5], part), 71), part)
    return {"queries": queries, "keys": keys, "values": values, "segments": segments, "partner": partner}


def one_batch(packed_rollout):
    query_matrix_rows, key_matrix_rows, value_rows, seg_rows = packed_rollout
    token_rows = query_matrix_rows.shape[0]
    groups_per_batch = QUERY_HEADS // KEY_VALUE_HEADS
    query_block_tile = query_matrix_rows.astype(jnp.float32).reshape(token_rows, KEY_VALUE_HEADS, groups_per_batch, HEAD_SIZE)
    key_block_tile = key_matrix_rows.astype(jnp.float32).reshape(token_rows, KEY_VALUE_HEADS, HEAD_SIZE)
    value_tile = value_rows.astype(jnp.float32).reshape(token_rows, KEY_VALUE_HEADS, HEAD_SIZE)
    scores = jnp.einsum("qkgd,tkd->qkgt", query_block_tile, key_block_tile) * (HEAD_SIZE ** -0.5)
    positions = jnp.arange(token_rows)
    allowed = (seg_rows[None, :] == seg_rows[:, None]) & (positions[None, :] <= positions[:, None])
    allowed = allowed[:, None, None, :]
    scores = jnp.where(allowed, scores, -1e30)
    top = jnp.max(scores, axis=-1, keepdims=True)
    terms = jnp.where(allowed, jnp.exp(scores - top), 0.0)
    total = jnp.sum(terms, axis=-1)
    weights = terms.astype(jnp.bfloat16).astype(jnp.float32)
    mixed = jnp.einsum("qkgt,tkd->qkgd", weights, value_tile) / total[..., None]
    return mixed.reshape(token_rows, QUERY_HEADS * HEAD_SIZE).astype(jnp.bfloat16)


def reference(queries, keys, values, segments, partner):
    micro_batch_rows = TOK_DEV
    packed_rollout = (queries.reshape(N_DP, micro_batch_rows, QUERY_HEADS * HEAD_SIZE), keys.reshape(N_DP, micro_batch_rows, KEY_VALUE_HEADS * HEAD_SIZE),
              values.reshape(N_DP, micro_batch_rows, KEY_VALUE_HEADS * HEAD_SIZE), segments.reshape(N_DP, micro_batch_rows))
    full = lax.map(one_batch, packed_rollout)
    quarters = full.reshape(N_DP, micro_batch_rows, 2, 2, QUERY_HEADS * HEAD_SIZE // 4)
    near = quarters[:, :, :, 0, :].reshape(N_DP * micro_batch_rows, QUERY_HEADS * HEAD_SIZE // 2)
    moved = jnp.take(quarters, partner.astype(jnp.int32), axis=0)
    lent = moved[:, :, :, 1, :].reshape(N_DP * micro_batch_rows, QUERY_HEADS * HEAD_SIZE // 2)
    return (near, lent)
```

```python
import functools
import math

import jax
import jax.numpy as jnp
from jax import lax
from jax.experimental import pallas as pl
from jax.experimental.pallas import tpu as pltpu
from jax.sharding import PartitionSpec as P

HEAD_SIZE = 128
SCORE_FACTOR = math.log2(math.e) / math.sqrt(HEAD_SIZE)


def attend_kernel(heads, seg_ref, query_ref, key_ref, value_ref, out_ref, bias_ref):
    tokens = query_ref.shape[0]
    half = tokens // 2
    key_segs = jnp.broadcast_to(seg_ref[...], (tokens, tokens))
    row = lax.broadcasted_iota(jnp.int32, (tokens, tokens), 0)
    col = lax.broadcasted_iota(jnp.int32, (tokens, tokens), 1)
    bias_ref[...] = jnp.where((key_segs == key_segs.T) & (col <= row), 0.0, -jnp.inf)
    for head in range(heads):
        cols = slice(head * HEAD_SIZE, (head + 1) * HEAD_SIZE)
        for start, seen in ((0, half), (half, tokens)):
            rows = slice(start, start + half)
            scores = lax.dot_general(
                query_ref[rows, cols],
                key_ref[:seen, :],
                (((1,), (1,)), ((), ())),
                preferred_element_type=jnp.float32,
            )
            scores = scores * SCORE_FACTOR + bias_ref[rows, :seen]
            terms = jnp.exp2(scores - jnp.max(scores, axis=1, keepdims=True))
            total = jnp.sum(terms, axis=1, keepdims=True)
            mixed = jnp.dot(
                terms.astype(jnp.bfloat16), value_ref[:seen, :], preferred_element_type=jnp.float32
            )
            out_ref[rows, cols] = (mixed / total).astype(jnp.bfloat16)


def attend(segments, queries, keys, values, kv_head):
    tokens = queries.shape[0]
    width = queries.shape[1] // (keys.shape[1] // HEAD_SIZE)
    heads = width // HEAD_SIZE
    return pl.pallas_call(
        functools.partial(attend_kernel, heads),
        grid=(1,),
        out_shape=jax.ShapeDtypeStruct((tokens, width), jnp.bfloat16),
        in_specs=[
            pl.BlockSpec((1, tokens), lambda i: (0, 0)),
            pl.BlockSpec((tokens, width), lambda i: (0, kv_head)),
            pl.BlockSpec((tokens, HEAD_SIZE), lambda i: (0, kv_head)),
            pl.BlockSpec((tokens, HEAD_SIZE), lambda i: (0, kv_head)),
        ],
        out_specs=pl.BlockSpec((tokens, width), lambda i: (0, 0)),
        scratch_shapes=[pltpu.VMEM((tokens, tokens), jnp.float32)],
        cost_estimate=pl.CostEstimate(
            flops=4 * tokens * tokens * width,
            bytes_accessed=4 * tokens * width,
            transcendentals=tokens * tokens * heads,
        ),
        compiler_params=pltpu.CompilerParams(vmem_limit_bytes=16 * 1024 * 1024),
    )(segments.reshape(1, tokens), queries, keys, values)


def per_device(queries, keys, values, segments, partner):
    ranks = lax.axis_size("dp")
    me = lax.axis_index("dp")
    second = attend(segments, queries, keys, values, 1)

    def swap(distance):
        pairs = [(rank, rank ^ distance) for rank in range(ranks)]

        def branch(second, queries, keys, values, segments):
            lent = lax.ppermute(second, "dp", pairs)
            near = attend(segments, queries, keys, values, 0)
            return near, lent

        return branch

    branches = [swap(distance) for distance in range(1, ranks)]
    choice = (me ^ lax.dynamic_index_in_dim(partner, me, keepdims=False)) - 1
    return lax.switch(choice, branches, second, queries, keys, values, segments)


def solution(mesh):
    rows = P(("groups", "dp"), "tensor")
    return jax.shard_map(
        per_device,
        mesh=mesh,
        in_specs=(rows, rows, rows, P(("groups", "dp")), P("groups")),
        out_specs=(rows, rows),
        check_vma=False,
    )
```

```python
import functools
import math

import jax
import jax.numpy as jnp
from jax import lax
from jax.experimental import pallas as pl
from jax.experimental.pallas import tpu as pltpu
from jax.sharding import PartitionSpec as P

HEAD_SIZE = 128
SCORE_FACTOR = math.log2(math.e) / math.sqrt(HEAD_SIZE)
FIRST_HEADS = 4


def fill_bias(seg_ref, bias_ref, first):
    rows, seen = bias_ref.shape
    row_segs = jnp.broadcast_to(seg_ref[:, first : first + rows], (rows, rows)).T
    row = first + lax.broadcasted_iota(jnp.int32, (rows, rows), 0)
    for start in range(0, seen, rows):
        key_segs = jnp.broadcast_to(seg_ref[:, start : start + rows], (rows, rows))
        col = start + lax.broadcasted_iota(jnp.int32, (rows, rows), 1)
        allowed = (key_segs == row_segs) & (col <= row)
        bias_ref[:, start : start + rows] = jnp.where(allowed, 0.0, -jnp.inf)


def attend_rows(query_ref, key_ref, value_ref, bias_ref, out_ref, rows):
    seen = bias_ref.shape[1]
    for start in range(0, query_ref.shape[1], HEAD_SIZE):
        cols = slice(start, start + HEAD_SIZE)
        scores = lax.dot_general(
            query_ref[rows, cols],
            key_ref[:seen, :],
            (((1,), (1,)), ((), ())),
            preferred_element_type=jnp.float32,
        )
        scores = scores * SCORE_FACTOR + bias_ref[...]
        terms = jnp.exp2(scores - jnp.max(scores, axis=1, keepdims=True))
        total = jnp.sum(terms, axis=1, keepdims=True)
        mixed = jnp.dot(
            terms.astype(jnp.bfloat16), value_ref[:seen, :], preferred_element_type=jnp.float32
        )
        out_ref[rows, cols] = (mixed / total).astype(jnp.bfloat16)


def attend_heads(seg_ref, query_ref, key_ref, value_ref, out_ref, bias_refs):
    half = query_ref.shape[0] // 2
    for index, bias_ref in enumerate(bias_refs):
        fill_bias(seg_ref, bias_ref, index * half)
    for index, bias_ref in enumerate(bias_refs):
        rows = slice(index * half, (index + 1) * half)
        attend_rows(query_ref, key_ref, value_ref, bias_ref, out_ref, rows)


def first_kernel(
    partner_hbm, seg_hbm, query_hbm, key_hbm, value_hbm, choice_ref, seg_ref, out_ref,
    partner_ref, query_ref, key_ref, value_ref, top_bias_ref, bottom_bias_ref, sems,
):
    start = query_hbm.shape[1] // 2
    heads = slice(start, start + out_ref.shape[1])
    head = slice(HEAD_SIZE, 2 * HEAD_SIZE)
    loads = [
        pltpu.make_async_copy(source, target, sems.at[index])
        for index, (source, target) in enumerate(
            (
                (partner_hbm, partner_ref),
                (seg_hbm, seg_ref),
                (key_hbm.at[:, head], key_ref),
                (query_hbm.at[:, heads], query_ref),
                (value_hbm.at[:, head], value_ref),
            )
        )
    ]
    for load in loads:
        load.start()
    for load in loads:
        load.wait()
    me = lax.axis_index("dp")
    choice_ref[0] = (me ^ partner_ref[me]) - 1
    attend_heads(seg_ref, query_ref, key_ref, value_ref, out_ref, (top_bias_ref, bottom_bias_ref))


def rest_kernel(skip, seg_ref, query_ref, key_ref, value_ref, out_ref, top_bias_ref, bottom_bias_ref):
    query_ref = query_ref.at[:, skip:]
    attend_heads(seg_ref, query_ref, key_ref, value_ref, out_ref, (top_bias_ref, bottom_bias_ref))


def params():
    return pltpu.CompilerParams(vmem_limit_bytes=16 * 1024 * 1024)


def cost(rows, width):
    return pl.CostEstimate(
        flops=4 * rows * rows * width,
        bytes_accessed=4 * rows * width,
        transcendentals=rows * rows * width // HEAD_SIZE,
    )


def biases(tokens):
    half = tokens // 2
    return [pltpu.VMEM((half, half), jnp.float32), pltpu.VMEM((half, tokens), jnp.float32)]


def attend_first(partner, seg_row, queries, keys, values, width):
    tokens = queries.shape[0]
    hbm = pl.BlockSpec(memory_space=pltpu.HBM)
    vmem = pl.BlockSpec(memory_space=pltpu.VMEM)
    operands = (partner, seg_row, queries, keys, values)
    return pl.pallas_call(
        first_kernel,
        out_shape=(
            pltpu.SMEM((1,), jnp.int32),
            pltpu.VMEM(seg_row.shape, jnp.int32),
            jax.ShapeDtypeStruct((tokens, width), jnp.bfloat16),
        ),
        in_specs=[hbm] * 5,
        out_specs=(pl.BlockSpec(memory_space=pltpu.SMEM), vmem, vmem),
        scratch_shapes=[
            pltpu.SMEM(partner.shape, jnp.int32),
            pltpu.VMEM((tokens, width), jnp.bfloat16),
            pltpu.VMEM((tokens, HEAD_SIZE), jnp.bfloat16),
            pltpu.VMEM((tokens, HEAD_SIZE), jnp.bfloat16),
        ]
        + biases(tokens)
        + [pltpu.SemaphoreType.DMA((5,))],
        cost_estimate=cost(tokens, width),
        compiler_params=params(),
    )(*(pltpu.with_memory_space_constraint(operand, pltpu.HBM) for operand in operands))


def attend_rest(seg_row, queries, keys, values, kv_head, skip):
    tokens = queries.shape[0]
    width = queries.shape[1] // 2
    return pl.pallas_call(
        functools.partial(rest_kernel, skip),
        grid=(1,),
        out_shape=jax.ShapeDtypeStruct((tokens, width - skip), jnp.bfloat16),
        in_specs=[
            pl.BlockSpec((1, tokens), lambda i: (0, 0)),
            pl.BlockSpec((tokens, width), lambda i: (0, kv_head)),
            pl.BlockSpec((tokens, HEAD_SIZE), lambda i: (0, kv_head)),
            pl.BlockSpec((tokens, HEAD_SIZE), lambda i: (0, kv_head)),
        ],
        out_specs=pl.BlockSpec((tokens, width - skip), lambda i: (0, 0)),
        scratch_shapes=biases(tokens),
        cost_estimate=cost(tokens, width - skip),
        compiler_params=params(),
    )(seg_row, queries, keys, values)


def place_kernel(first, part_ref, *refs):
    out_ref, sem = refs[-2:]
    copy = pltpu.make_async_copy(part_ref, out_ref.at[:, pl.ds(first, part_ref.shape[1])], sem)
    copy.start()
    copy.wait()


def place(part, first, width, whole=None):
    operands = (part,) if whole is None else (part, whole)
    return pl.pallas_call(
        functools.partial(place_kernel, first),
        out_shape=pltpu.HBM((part.shape[0], width), part.dtype),
        in_specs=[pl.BlockSpec(memory_space=pl.ANY), pl.BlockSpec(memory_space=pltpu.HBM)][: len(operands)],
        out_specs=pl.BlockSpec(memory_space=pltpu.HBM),
        scratch_shapes=[pltpu.SemaphoreType.DMA],
        input_output_aliases={} if whole is None else {1: 0},
        cost_estimate=pl.CostEstimate(flops=0, bytes_accessed=4 * part.size, transcendentals=0),
        compiler_params=params(),
    )(*operands)


def per_device(queries, keys, values, segments, partner):
    tokens = queries.shape[0]
    width = queries.shape[1] // 2
    early = FIRST_HEADS * HEAD_SIZE
    ranks = lax.axis_size("dp")
    choice, seg_row, first = attend_first(partner, segments.reshape(1, tokens), queries, keys, values, early)

    def swap(distance):
        pairs = [(rank, rank ^ distance) for rank in range(ranks)]

        def branch(first, queries, keys, values, seg_row):
            first_lent = lax.ppermute(first, "dp", pairs)
            rest_lent = lax.ppermute(attend_rest(seg_row, queries, keys, values, 1, early), "dp", pairs)
            near = attend_rest(seg_row, queries, keys, values, 0, 0)
            return near, place(rest_lent, early, width, place(first_lent, 0, width))

        return branch

    branches = [swap(distance) for distance in range(1, ranks)]
    return lax.switch(choice[0], branches, first, queries, keys, values, seg_row)


def solution(mesh):
    rows = P(("groups", "dp"), "tensor")
    return jax.shard_map(
        per_device,
        mesh=mesh,
        in_specs=(rows, rows, rows, P(("groups", "dp")), P("groups")),
        out_specs=(rows, rows),
        check_vma=False,
    )
```

```python
import functools
import math

import jax
import jax.numpy as jnp
from jax import lax
from jax.experimental import pallas as pl
from jax.experimental.pallas import tpu as pltpu
from jax.sharding import PartitionSpec as P

HEAD_SIZE = 128
SCORE_FACTOR = math.log2(math.e) / math.sqrt(HEAD_SIZE)
PARTS = 2
MOST_SWITCHED = 8


def fill_bias(seg_ref, bias_ref, first):
    rows, seen = bias_ref.shape
    row_segs = jnp.broadcast_to(seg_ref[:, first : first + rows], (rows, rows)).T
    row = first + lax.broadcasted_iota(jnp.int32, (rows, rows), 0)
    for start in range(0, seen, rows):
        key_segs = jnp.broadcast_to(seg_ref[:, start : start + rows], (rows, rows))
        col = start + lax.broadcasted_iota(jnp.int32, (rows, rows), 1)
        allowed = (key_segs == row_segs) & (col <= row)
        bias_ref[:, start : start + rows] = jnp.where(allowed, 0.0, -jnp.inf)


def attend_rows(query_ref, key_ref, value_ref, bias_ref, out_ref, rows):
    seen = bias_ref.shape[1]
    for start in range(0, query_ref.shape[1], HEAD_SIZE):
        cols = slice(start, start + HEAD_SIZE)
        scores = lax.dot_general(
            query_ref[rows, cols],
            key_ref[:seen, :],
            (((1,), (1,)), ((), ())),
            preferred_element_type=jnp.float32,
        )
        scores = scores * SCORE_FACTOR + bias_ref[...]
        terms = jnp.exp2(scores - jnp.max(scores, axis=1, keepdims=True))
        total = jnp.sum(terms, axis=1, keepdims=True)
        mixed = jnp.dot(
            terms.astype(jnp.bfloat16), value_ref[:seen, :], preferred_element_type=jnp.float32
        )
        out_ref[rows, cols] = (mixed / total).astype(jnp.bfloat16)


def attend_heads(seg_ref, query_ref, key_ref, value_ref, out_ref, bias_refs):
    half = query_ref.shape[0] // 2
    for index, bias_ref in enumerate(bias_refs):
        fill_bias(seg_ref, bias_ref, index * half)
    for index, bias_ref in enumerate(bias_refs):
        rows = slice(index * half, (index + 1) * half)
        attend_rows(query_ref, key_ref, value_ref, bias_ref, out_ref, rows)


def first_kernel(
    partner_hbm, seg_hbm, query_hbm, key_hbm, value_hbm, choice_ref, seg_ref, out_ref,
    partner_ref, query_ref, key_ref, value_ref, top_bias_ref, bottom_bias_ref, sems,
):
    start = query_hbm.shape[1] // 2
    heads = slice(start, start + out_ref.shape[1])
    head = slice(HEAD_SIZE, 2 * HEAD_SIZE)
    loads = [
        pltpu.make_async_copy(source, target, sems.at[index])
        for index, (source, target) in enumerate(
            (
                (partner_hbm, partner_ref),
                (seg_hbm, seg_ref),
                (key_hbm.at[:, head], key_ref),
                (query_hbm.at[:, heads], query_ref),
                (value_hbm.at[:, head], value_ref),
            )
        )
    ]
    for load in loads:
        load.start()
    for load in loads:
        load.wait()
    me = lax.axis_index("dp")
    choice_ref[0] = (me ^ partner_ref[me]) - 1
    attend_heads(seg_ref, query_ref, key_ref, value_ref, out_ref, (top_bias_ref, bottom_bias_ref))


def part_kernel(seg_ref, query_ref, key_ref, value_ref, out_ref, top_bias_ref, bottom_bias_ref):
    attend_heads(seg_ref, query_ref, key_ref, value_ref, out_ref, (top_bias_ref, bottom_bias_ref))


def params():
    return pltpu.CompilerParams(vmem_limit_bytes=16 * 1024 * 1024)


def cost(rows, width):
    return pl.CostEstimate(
        flops=4 * rows * rows * width,
        bytes_accessed=4 * rows * width,
        transcendentals=rows * rows * width // HEAD_SIZE,
    )


def biases(tokens):
    half = tokens // 2
    return [pltpu.VMEM((half, half), jnp.float32), pltpu.VMEM((half, tokens), jnp.float32)]


def attend_first(partner, seg_row, queries, keys, values, width):
    tokens = queries.shape[0]
    hbm = pl.BlockSpec(memory_space=pltpu.HBM)
    vmem = pl.BlockSpec(memory_space=pltpu.VMEM)
    operands = (partner, seg_row, queries, keys, values)
    return pl.pallas_call(
        first_kernel,
        out_shape=(
            pltpu.SMEM((1,), jnp.int32),
            pltpu.VMEM(seg_row.shape, jnp.int32),
            jax.ShapeDtypeStruct((tokens, width), jnp.bfloat16),
        ),
        in_specs=[hbm] * 5,
        out_specs=(pl.BlockSpec(memory_space=pltpu.SMEM), vmem, vmem),
        scratch_shapes=[
            pltpu.SMEM(partner.shape, jnp.int32),
            pltpu.VMEM((tokens, width), jnp.bfloat16),
            pltpu.VMEM((tokens, HEAD_SIZE), jnp.bfloat16),
            pltpu.VMEM((tokens, HEAD_SIZE), jnp.bfloat16),
        ]
        + biases(tokens)
        + [pltpu.SemaphoreType.DMA((5,))],
        cost_estimate=cost(tokens, width),
        compiler_params=params(),
    )(*(pltpu.with_memory_space_constraint(operand, pltpu.HBM) for operand in operands))


def attend_part(seg_row, queries, keys, values, kv_head, part, parts):
    tokens = queries.shape[0]
    width = queries.shape[1] // 2 // parts
    return pl.pallas_call(
        part_kernel,
        grid=(1,),
        out_shape=jax.ShapeDtypeStruct((tokens, width), jnp.bfloat16),
        in_specs=[
            pl.BlockSpec((1, tokens), lambda i: (0, 0)),
            pl.BlockSpec((tokens, width), lambda i: (0, kv_head * parts + part)),
            pl.BlockSpec((tokens, HEAD_SIZE), lambda i: (0, kv_head)),
            pl.BlockSpec((tokens, HEAD_SIZE), lambda i: (0, kv_head)),
        ],
        out_specs=pl.BlockSpec((tokens, width), lambda i: (0, 0)),
        scratch_shapes=biases(tokens),
        cost_estimate=cost(tokens, width),
        compiler_params=params(),
    )(seg_row, *(pltpu.with_memory_space_constraint(one, pltpu.HBM) for one in (queries, keys, values)))


def place_kernel(first, part_ref, *refs):
    out_ref, sem = refs[-2:]
    copy = pltpu.make_async_copy(part_ref, out_ref.at[:, pl.ds(first, part_ref.shape[1])], sem)
    copy.start()
    copy.wait()


def place(part, first, width, whole=None):
    operands = (part,) if whole is None else (part, whole)
    return pl.pallas_call(
        functools.partial(place_kernel, first),
        out_shape=pltpu.HBM((part.shape[0], width), part.dtype),
        in_specs=[pl.BlockSpec(memory_space=pl.ANY), pl.BlockSpec(memory_space=pltpu.HBM)][: len(operands)],
        out_specs=pl.BlockSpec(memory_space=pltpu.HBM),
        scratch_shapes=[pltpu.SemaphoreType.DMA],
        input_output_aliases={} if whole is None else {1: 0},
        cost_estimate=pl.CostEstimate(flops=0, bytes_accessed=4 * part.size, transcendentals=0),
        compiler_params=params(),
    )(*operands)


def per_device(queries, keys, values, segments, partner):
    tokens = queries.shape[0]
    width = queries.shape[1] // 2
    ranks = lax.axis_size("dp")
    seg_row = segments.reshape(1, tokens)
    if ranks > MOST_SWITCHED:
        second = attend_part(seg_row, queries, keys, values, 1, 0, 1)
        slots = second.reshape(ranks, 1, second.size // ranks)
        spread = lax.all_to_all(slots, "dp", split_axis=0, concat_axis=0, tiled=True)
        onward = jnp.take(spread, partner, axis=0)
        arrived = lax.all_to_all(onward, "dp", split_axis=0, concat_axis=0, tiled=True)
        near = attend_part(seg_row, queries, keys, values, 0, 0, 1)
        return near, arrived.reshape(second.shape)

    choice, seg_row, first = attend_first(partner, seg_row, queries, keys, values, width // PARTS)

    def swap(distance):
        pairs = [(rank, rank ^ distance) for rank in range(ranks)]

        def branch(first, queries, keys, values, seg_row):
            arrived = [lax.ppermute(first, "dp", pairs)]
            for part in range(1, PARTS):
                heads = attend_part(seg_row, queries, keys, values, 1, part, PARTS)
                arrived.append(lax.ppermute(heads, "dp", pairs))
            near = attend_part(seg_row, queries, keys, values, 0, 0, 1)
            lent = None
            for part, heads in enumerate(arrived):
                lent = place(heads, part * heads.shape[1], width, lent)
            return near, lent

        return branch

    branches = [swap(distance) for distance in range(1, ranks)]
    return lax.switch(choice[0], branches, first, queries, keys, values, seg_row)


def solution(mesh):
    rows = P(("groups", "dp"), "tensor")
    return jax.shard_map(
        per_device,
        mesh=mesh,
        in_specs=(rows, rows, rows, P(("groups", "dp")), P("groups")),
        out_specs=(rows, rows),
        check_vma=False,
    )
```

```python
import functools
import math

import jax
import jax.numpy as jnp
from jax import lax
from jax.experimental import pallas as pl
from jax.experimental.pallas import tpu as pltpu
from jax.sharding import PartitionSpec as P

HEAD_SIZE = 128
SCORE_FACTOR = math.log2(math.e) / math.sqrt(HEAD_SIZE)
HEAD_PARTS = (2, 6)
MOST_SWITCHED = 8


def fill_bias(seg_ref, bias_ref, first):
    rows, seen = bias_ref.shape
    row_segs = jnp.broadcast_to(seg_ref[:, first : first + rows], (rows, rows)).T
    row = first + lax.broadcasted_iota(jnp.int32, (rows, rows), 0)
    for start in range(0, seen, rows):
        key_segs = jnp.broadcast_to(seg_ref[:, start : start + rows], (rows, rows))
        col = start + lax.broadcasted_iota(jnp.int32, (rows, rows), 1)
        allowed = (key_segs == row_segs) & (col <= row)
        bias_ref[:, start : start + rows] = jnp.where(allowed, 0.0, -jnp.inf)


def attend_rows(query_ref, key_ref, value_ref, bias_ref, out_ref, rows):
    seen = bias_ref.shape[1]
    for start in range(0, query_ref.shape[1], HEAD_SIZE):
        cols = slice(start, start + HEAD_SIZE)
        scores = lax.dot_general(
            query_ref[rows, cols],
            key_ref[:seen, :],
            (((1,), (1,)), ((), ())),
            preferred_element_type=jnp.float32,
        )
        scores = scores * SCORE_FACTOR + bias_ref[...]
        terms = jnp.exp2(scores - jnp.max(scores, axis=1, keepdims=True))
        total = jnp.sum(terms, axis=1, keepdims=True)
        mixed = jnp.dot(
            terms.astype(jnp.bfloat16), value_ref[:seen, :], preferred_element_type=jnp.float32
        )
        out_ref[rows, cols] = (mixed / total).astype(jnp.bfloat16)


def fill_biases(seg_ref, bias_refs):
    for index, bias_ref in enumerate(bias_refs):
        fill_bias(seg_ref, bias_ref, index * bias_ref.shape[0])


def attend_heads(query_ref, key_ref, value_ref, out_ref, bias_refs):
    half = query_ref.shape[0] // 2
    for index, bias_ref in enumerate(bias_refs):
        rows = slice(index * half, (index + 1) * half)
        attend_rows(query_ref, key_ref, value_ref, bias_ref, out_ref, rows)


def first_kernel(
    partner_hbm, seg_hbm, query_hbm, key_hbm, value_hbm,
    choice_ref, seg_ref, key_ref, value_ref, later_ref, out_ref,
    partner_ref, query_ref, top_bias_ref, bottom_bias_ref, sems,
):
    start = query_hbm.shape[1] // 2
    split = start + out_ref.shape[1]
    head = slice(HEAD_SIZE, 2 * HEAD_SIZE)
    loads = [
        pltpu.make_async_copy(source, target, sems.at[index])
        for index, (source, target) in enumerate(
            (
                (partner_hbm, partner_ref),
                (seg_hbm, seg_ref),
                (key_hbm.at[:, head], key_ref),
                (query_hbm.at[:, start:split], query_ref),
                (value_hbm.at[:, head], value_ref),
                (query_hbm.at[:, split:], later_ref),
            )
        )
    ]
    for load in loads:
        load.start()
    for load in loads[:2]:
        load.wait()
    me = lax.axis_index("dp")
    choice_ref[0] = (me ^ partner_ref[me]) - 1
    fill_biases(seg_ref, (top_bias_ref, bottom_bias_ref))
    for load in loads[2:5]:
        load.wait()
    attend_heads(query_ref, key_ref, value_ref, out_ref, (top_bias_ref, bottom_bias_ref))
    loads[5].wait()


def later_kernel(cols, seg_ref, query_ref, key_ref, value_ref, out_ref, top_bias_ref, bottom_bias_ref):
    fill_biases(seg_ref, (top_bias_ref, bottom_bias_ref))
    query_ref = query_ref.at[:, cols]
    attend_heads(query_ref, key_ref, value_ref, out_ref, (top_bias_ref, bottom_bias_ref))


def part_kernel(skip, seg_ref, query_ref, key_ref, value_ref, out_ref, top_bias_ref, bottom_bias_ref):
    query_ref = query_ref.at[:, skip:]
    fill_biases(seg_ref, (top_bias_ref, bottom_bias_ref))
    attend_heads(query_ref, key_ref, value_ref, out_ref, (top_bias_ref, bottom_bias_ref))


def params():
    return pltpu.CompilerParams(vmem_limit_bytes=16 * 1024 * 1024)


def cost(rows, width):
    return pl.CostEstimate(
        flops=4 * rows * rows * width,
        bytes_accessed=4 * rows * width,
        transcendentals=rows * rows * width // HEAD_SIZE,
    )


def biases(tokens):
    half = tokens // 2
    return [pltpu.VMEM((half, half), jnp.float32), pltpu.VMEM((half, tokens), jnp.float32)]


def attend_first(partner, seg_row, queries, keys, values, width):
    tokens = queries.shape[0]
    hbm = pl.BlockSpec(memory_space=pltpu.HBM)
    vmem = pl.BlockSpec(memory_space=pltpu.VMEM)
    operands = (partner, seg_row, queries, keys, values)
    return pl.pallas_call(
        first_kernel,
        out_shape=(
            pltpu.SMEM((1,), jnp.int32),
            pltpu.VMEM(seg_row.shape, jnp.int32),
            pltpu.VMEM((tokens, HEAD_SIZE), jnp.bfloat16),
            pltpu.VMEM((tokens, HEAD_SIZE), jnp.bfloat16),
            pltpu.VMEM((tokens, queries.shape[1] // 2 - width), jnp.bfloat16),
            jax.ShapeDtypeStruct((tokens, width), jnp.bfloat16),
        ),
        in_specs=[hbm] * 5,
        out_specs=(pl.BlockSpec(memory_space=pltpu.SMEM),) + (vmem,) * 5,
        scratch_shapes=[
            pltpu.SMEM(partner.shape, jnp.int32),
            pltpu.VMEM((tokens, width), jnp.bfloat16),
        ]
        + biases(tokens)
        + [pltpu.SemaphoreType.DMA((6,))],
        cost_estimate=cost(tokens, width),
        compiler_params=params(),
    )(*(pltpu.with_memory_space_constraint(operand, pltpu.HBM) for operand in operands))


def attend_later(seg_row, later, key, value, start, width):
    tokens = later.shape[0]
    vmem = pl.BlockSpec(memory_space=pltpu.VMEM)
    return pl.pallas_call(
        functools.partial(later_kernel, slice(start, start + width)),
        out_shape=jax.ShapeDtypeStruct((tokens, width), jnp.bfloat16),
        in_specs=[vmem] * 4,
        out_specs=vmem,
        scratch_shapes=biases(tokens),
        cost_estimate=cost(tokens, width),
        compiler_params=params(),
    )(seg_row, later, key, value)


def attend_rest(seg_row, queries, keys, values, kv_head, skip):
    tokens = queries.shape[0]
    width = queries.shape[1] // 2
    return pl.pallas_call(
        functools.partial(part_kernel, skip),
        grid=(1,),
        out_shape=jax.ShapeDtypeStruct((tokens, width - skip), jnp.bfloat16),
        in_specs=[
            pl.BlockSpec((1, tokens), lambda i: (0, 0)),
            pl.BlockSpec((tokens, width), lambda i: (0, kv_head)),
            pl.BlockSpec((tokens, HEAD_SIZE), lambda i: (0, kv_head)),
            pl.BlockSpec((tokens, HEAD_SIZE), lambda i: (0, kv_head)),
        ],
        out_specs=pl.BlockSpec((tokens, width - skip), lambda i: (0, 0)),
        scratch_shapes=biases(tokens),
        cost_estimate=cost(tokens, width - skip),
        compiler_params=params(),
    )(seg_row, *(pltpu.with_memory_space_constraint(one, pltpu.HBM) for one in (queries, keys, values)))


def place_kernel(first, part_ref, *refs):
    out_ref, sem = refs[-2:]
    copy = pltpu.make_async_copy(part_ref, out_ref.at[:, pl.ds(first, part_ref.shape[1])], sem)
    copy.start()
    copy.wait()


def place(part, first, width, whole=None):
    operands = (part,) if whole is None else (part, whole)
    return pl.pallas_call(
        functools.partial(place_kernel, first),
        out_shape=pltpu.HBM((part.shape[0], width), part.dtype),
        in_specs=[pl.BlockSpec(memory_space=pl.ANY), pl.BlockSpec(memory_space=pltpu.HBM)][: len(operands)],
        out_specs=pl.BlockSpec(memory_space=pltpu.HBM),
        scratch_shapes=[pltpu.SemaphoreType.DMA],
        input_output_aliases={} if whole is None else {1: 0},
        cost_estimate=pl.CostEstimate(flops=10**10, bytes_accessed=2**28, transcendentals=0),
        compiler_params=params(),
    )(*operands)


def per_device(queries, keys, values, segments, partner):
    tokens = queries.shape[0]
    width = queries.shape[1] // 2
    ranks = lax.axis_size("dp")
    seg_row = segments.reshape(1, tokens)
    if ranks > MOST_SWITCHED:
        second = attend_rest(seg_row, queries, keys, values, 1, 0)
        slots = second.reshape(ranks, 1, second.size // ranks)
        spread = lax.all_to_all(slots, "dp", split_axis=0, concat_axis=0, tiled=True)
        onward = jnp.take(spread, partner, axis=0)
        arrived = lax.all_to_all(onward, "dp", split_axis=0, concat_axis=0, tiled=True)
        near = attend_rest(seg_row, queries, keys, values, 0, 0)
        return near, arrived.reshape(second.shape)

    widths = [heads * HEAD_SIZE for heads in HEAD_PARTS]
    choice, seg_row, key, value, later, first = attend_first(
        partner, seg_row, queries, keys, values, widths[0]
    )

    def swap(distance):
        pairs = [(rank, rank ^ distance) for rank in range(ranks)]

        def branch(first, later, key, value, seg_row, queries, keys, values):
            arrived = [lax.ppermute(first, "dp", pairs)]
            start = 0
            for part in widths[1:]:
                heads = attend_later(seg_row, later, key, value, start, part)
                arrived.append(lax.ppermute(heads, "dp", pairs))
                start += part
            near = attend_rest(seg_row, queries, keys, values, 0, 0)
            lent, start = None, 0
            for heads, part in zip(arrived, widths):
                lent = place(heads, start, width, lent)
                start += part
            return near, lent

        return branch

    branches = [swap(distance) for distance in range(1, ranks)]
    return lax.switch(choice[0], branches, first, later, key, value, seg_row, queries, keys, values)


def solution(mesh):
    rows = P(("groups", "dp"), "tensor")
    return jax.shard_map(
        per_device,
        mesh=mesh,
        in_specs=(rows, rows, rows, P(("groups", "dp")), P("groups")),
        out_specs=(rows, rows),
        check_vma=False,
    )
```

```python
import functools
import math

import jax
import jax.numpy as jnp
from jax import lax
from jax.experimental import pallas as pl
from jax.experimental.pallas import tpu as pltpu
from jax.sharding import PartitionSpec as P

HEAD_SIZE = 128
SCORE_FACTOR = math.log2(math.e) / math.sqrt(HEAD_SIZE)
PARTS = 2
MOST_SWITCHED = 8


def fill_bias(seg_ref, bias_ref, first):
    rows, seen = bias_ref.shape
    row_segs = jnp.broadcast_to(seg_ref[:, first : first + rows], (rows, rows)).T
    row = first + lax.broadcasted_iota(jnp.int32, (rows, rows), 0)
    for start in range(0, seen, rows):
        key_segs = jnp.broadcast_to(seg_ref[:, start : start + rows], (rows, rows))
        col = start + lax.broadcasted_iota(jnp.int32, (rows, rows), 1)
        allowed = (key_segs == row_segs) & (col <= row)
        bias_ref[:, start : start + rows] = jnp.where(allowed, 0.0, -jnp.inf)


def attend_head(query_ref, key_ref, value_ref, bias_ref, out_ref, rows, cols):
    seen = bias_ref.shape[1]
    scores = lax.dot_general(
        query_ref[rows, cols],
        key_ref[:seen, :],
        (((1,), (1,)), ((), ())),
        preferred_element_type=jnp.float32,
    )
    scores = scores * SCORE_FACTOR + bias_ref[...]
    terms = jnp.exp2(scores - jnp.max(scores, axis=1, keepdims=True))
    total = jnp.sum(terms, axis=1, keepdims=True)
    mixed = jnp.dot(
        terms.astype(jnp.bfloat16), value_ref[:seen, :], preferred_element_type=jnp.float32
    )
    out_ref[rows, cols] = (mixed / total).astype(jnp.bfloat16)


def attend_heads(seg_ref, query_ref, key_ref, value_ref, out_ref, bias_refs, rolled=False):
    half = query_ref.shape[0] // 2
    heads = query_ref.shape[1] // HEAD_SIZE
    for index, bias_ref in enumerate(bias_refs):
        fill_bias(seg_ref, bias_ref, index * half)

    def attend_both(cols):
        for index, bias_ref in enumerate(bias_refs):
            rows = slice(index * half, (index + 1) * half)
            attend_head(query_ref, key_ref, value_ref, bias_ref, out_ref, rows, cols)

    if rolled:

        @pl.loop(0, heads)
        def _(head):
            attend_both(pl.ds(pl.multiple_of(head * HEAD_SIZE, HEAD_SIZE), HEAD_SIZE))

    else:
        for head in range(heads):
            attend_both(slice(head * HEAD_SIZE, (head + 1) * HEAD_SIZE))


def first_kernel(
    partner_hbm, seg_hbm, query_hbm, key_hbm, value_hbm, choice_ref, seg_ref, out_ref,
    partner_ref, query_ref, key_ref, value_ref, top_bias_ref, bottom_bias_ref, sems,
):
    start = query_hbm.shape[1] // 2
    heads = slice(start, start + out_ref.shape[1])
    head = slice(HEAD_SIZE, 2 * HEAD_SIZE)
    loads = [
        pltpu.make_async_copy(source, target, sems.at[index])
        for index, (source, target) in enumerate(
            (
                (partner_hbm, partner_ref),
                (seg_hbm, seg_ref),
                (key_hbm.at[:, head], key_ref),
                (query_hbm.at[:, heads], query_ref),
                (value_hbm.at[:, head], value_ref),
            )
        )
    ]
    for load in loads:
        load.start()
    for load in loads:
        load.wait()
    me = lax.axis_index("dp")
    choice_ref[0] = (me ^ partner_ref[me]) - 1
    attend_heads(seg_ref, query_ref, key_ref, value_ref, out_ref, (top_bias_ref, bottom_bias_ref))


def part_kernel(rolled, seg_ref, query_ref, key_ref, value_ref, out_ref, top_bias_ref, bottom_bias_ref):
    bias_refs = (top_bias_ref, bottom_bias_ref)
    attend_heads(seg_ref, query_ref, key_ref, value_ref, out_ref, bias_refs, rolled)


def params():
    return pltpu.CompilerParams(vmem_limit_bytes=16 * 1024 * 1024)


def cost(rows, width):
    return pl.CostEstimate(
        flops=4 * rows * rows * width,
        bytes_accessed=4 * rows * width,
        transcendentals=rows * rows * width // HEAD_SIZE,
    )


def biases(tokens):
    half = tokens // 2
    return [pltpu.VMEM((half, half), jnp.float32), pltpu.VMEM((half, tokens), jnp.float32)]


def attend_first(partner, seg_row, queries, keys, values, width):
    tokens = queries.shape[0]
    hbm = pl.BlockSpec(memory_space=pltpu.HBM)
    vmem = pl.BlockSpec(memory_space=pltpu.VMEM)
    operands = (partner, seg_row, queries, keys, values)
    return pl.pallas_call(
        first_kernel,
        out_shape=(
            pltpu.SMEM((1,), jnp.int32),
            pltpu.VMEM(seg_row.shape, jnp.int32),
            jax.ShapeDtypeStruct((tokens, width), jnp.bfloat16),
        ),
        in_specs=[hbm] * 5,
        out_specs=(pl.BlockSpec(memory_space=pltpu.SMEM), vmem, vmem),
        scratch_shapes=[
            pltpu.SMEM(partner.shape, jnp.int32),
            pltpu.VMEM((tokens, width), jnp.bfloat16),
            pltpu.VMEM((tokens, HEAD_SIZE), jnp.bfloat16),
            pltpu.VMEM((tokens, HEAD_SIZE), jnp.bfloat16),
        ]
        + biases(tokens)
        + [pltpu.SemaphoreType.DMA((5,))],
        cost_estimate=cost(tokens, width),
        compiler_params=params(),
    )(*(pltpu.with_memory_space_constraint(operand, pltpu.HBM) for operand in operands))


def attend_part(seg_row, queries, keys, values, kv_head, part, parts, rolled=False):
    tokens = queries.shape[0]
    width = queries.shape[1] // 2 // parts
    return pl.pallas_call(
        functools.partial(part_kernel, rolled),
        grid=(1,),
        out_shape=jax.ShapeDtypeStruct((tokens, width), jnp.bfloat16),
        in_specs=[
            pl.BlockSpec((1, tokens), lambda i: (0, 0)),
            pl.BlockSpec((tokens, width), lambda i: (0, kv_head * parts + part)),
            pl.BlockSpec((tokens, HEAD_SIZE), lambda i: (0, kv_head)),
            pl.BlockSpec((tokens, HEAD_SIZE), lambda i: (0, kv_head)),
        ],
        out_specs=pl.BlockSpec((tokens, width), lambda i: (0, 0)),
        scratch_shapes=biases(tokens),
        cost_estimate=cost(tokens, width),
        compiler_params=params(),
    )(seg_row, *(pltpu.with_memory_space_constraint(one, pltpu.HBM) for one in (queries, keys, values)))


def place_kernel(first, part_ref, *refs):
    out_ref, sem = refs[-2:]
    copy = pltpu.make_async_copy(part_ref, out_ref.at[:, pl.ds(first, part_ref.shape[1])], sem)
    copy.start()
    copy.wait()


def place(part, first, width, whole=None):
    operands = (part,) if whole is None else (part, whole)
    return pl.pallas_call(
        functools.partial(place_kernel, first),
        out_shape=pltpu.HBM((part.shape[0], width), part.dtype),
        in_specs=[pl.BlockSpec(memory_space=pl.ANY), pl.BlockSpec(memory_space=pltpu.HBM)][: len(operands)],
        out_specs=pl.BlockSpec(memory_space=pltpu.HBM),
        scratch_shapes=[pltpu.SemaphoreType.DMA],
        input_output_aliases={} if whole is None else {1: 0},
        cost_estimate=pl.CostEstimate(flops=0, bytes_accessed=4 * part.size, transcendentals=0),
        compiler_params=params(),
    )(*operands)


def per_device(queries, keys, values, segments, partner):
    tokens = queries.shape[0]
    width = queries.shape[1] // 2
    ranks = lax.axis_size("dp")
    seg_row = segments.reshape(1, tokens)
    if ranks > MOST_SWITCHED:
        second = attend_part(seg_row, queries, keys, values, 1, 0, 1)
        slots = second.reshape(ranks, 1, second.size // ranks)
        spread = lax.all_to_all(slots, "dp", split_axis=0, concat_axis=0, tiled=True)
        onward = jnp.take(spread, partner, axis=0)
        arrived = lax.all_to_all(onward, "dp", split_axis=0, concat_axis=0, tiled=True)
        near = attend_part(seg_row, queries, keys, values, 0, 0, 1)
        return near, arrived.reshape(second.shape)

    choice, seg_row, first = attend_first(partner, seg_row, queries, keys, values, width // PARTS)

    def swap(distance):
        pairs = [(rank, rank ^ distance) for rank in range(ranks)]

        def branch(first, queries, keys, values, seg_row):
            arrived = [lax.ppermute(first, "dp", pairs)]
            for part in range(1, PARTS):
                heads = attend_part(seg_row, queries, keys, values, 1, part, PARTS)
                arrived.append(lax.ppermute(heads, "dp", pairs))
            near = attend_part(seg_row, queries, keys, values, 0, 0, 1, rolled=True)
            lent = None
            for part, heads in enumerate(arrived):
                lent = place(heads, part * heads.shape[1], width, lent)
            return near, lent

        return branch

    branches = [swap(distance) for distance in range(1, ranks)]
    return lax.switch(choice[0], branches, first, queries, keys, values, seg_row)


def solution(mesh):
    rows = P(("groups", "dp"), "tensor")
    return jax.shard_map(
        per_device,
        mesh=mesh,
        in_specs=(rows, rows, rows, P(("groups", "dp")), P("groups")),
        out_specs=(rows, rows),
        check_vma=False,
    )
```

```python
import functools
import math

import jax
import jax.numpy as jnp
from jax import lax
from jax.experimental import pallas as pl
from jax.experimental.pallas import tpu as pltpu
from jax.sharding import PartitionSpec as P

HEAD_SIZE = 128
SCORE_FACTOR = math.log2(math.e) / math.sqrt(HEAD_SIZE)
HEAD_PARTS = (2, 6)
MOST_SWITCHED = 8


def fill_bias(seg_ref, bias_ref, first):
    rows, seen = bias_ref.shape
    row_segs = jnp.broadcast_to(seg_ref[:, first : first + rows], (rows, rows)).T
    row = first + lax.broadcasted_iota(jnp.int32, (rows, rows), 0)
    for start in range(0, seen, rows):
        key_segs = jnp.broadcast_to(seg_ref[:, start : start + rows], (rows, rows))
        col = start + lax.broadcasted_iota(jnp.int32, (rows, rows), 1)
        allowed = (key_segs == row_segs) & (col <= row)
        bias_ref[:, start : start + rows] = jnp.where(allowed, 0.0, -jnp.inf)


def attend_head(query_ref, key_ref, value_ref, bias_ref, out_ref, rows, cols):
    seen = bias_ref.shape[1]
    scores = lax.dot_general(
        query_ref[rows, cols],
        key_ref[:seen, :],
        (((1,), (1,)), ((), ())),
        preferred_element_type=jnp.float32,
    )
    scores = scores * SCORE_FACTOR + bias_ref[...]
    terms = jnp.exp2(scores - jnp.max(scores, axis=1, keepdims=True))
    total = jnp.sum(terms, axis=1, keepdims=True)
    mixed = jnp.dot(
        terms.astype(jnp.bfloat16), value_ref[:seen, :], preferred_element_type=jnp.float32
    )
    out_ref[rows, cols] = (mixed / total).astype(jnp.bfloat16)


def fill_biases(seg_ref, bias_refs):
    for index, bias_ref in enumerate(bias_refs):
        fill_bias(seg_ref, bias_ref, index * bias_ref.shape[0])


def attend_heads(query_ref, key_ref, value_ref, out_ref, bias_refs, rolled=False):
    half = query_ref.shape[0] // 2
    heads = query_ref.shape[1] // HEAD_SIZE

    def attend_both(cols):
        for index, bias_ref in enumerate(bias_refs):
            rows = slice(index * half, (index + 1) * half)
            attend_head(query_ref, key_ref, value_ref, bias_ref, out_ref, rows, cols)

    if rolled:

        @pl.loop(0, heads)
        def _(head):
            attend_both(pl.ds(pl.multiple_of(head * HEAD_SIZE, HEAD_SIZE), HEAD_SIZE))

    else:
        for head in range(heads):
            attend_both(slice(head * HEAD_SIZE, (head + 1) * HEAD_SIZE))


def first_kernel(
    partner_hbm, seg_hbm, query_hbm, key_hbm, value_hbm,
    choice_ref, seg_ref, key_ref, value_ref, later_ref, out_ref,
    partner_ref, query_ref, top_bias_ref, bottom_bias_ref, sems,
):
    start = query_hbm.shape[1] // 2
    split = start + out_ref.shape[1]
    head = slice(HEAD_SIZE, 2 * HEAD_SIZE)
    loads = [
        pltpu.make_async_copy(source, target, sems.at[index])
        for index, (source, target) in enumerate(
            (
                (partner_hbm, partner_ref),
                (seg_hbm, seg_ref),
                (key_hbm.at[:, head], key_ref),
                (query_hbm.at[:, start:split], query_ref),
                (value_hbm.at[:, head], value_ref),
                (query_hbm.at[:, split:], later_ref),
            )
        )
    ]
    for load in loads:
        load.start()
    for load in loads[:2]:
        load.wait()
    me = lax.axis_index("dp")
    choice_ref[0] = (me ^ partner_ref[me]) - 1
    fill_biases(seg_ref, (top_bias_ref, bottom_bias_ref))
    for load in loads[2:5]:
        load.wait()
    attend_heads(query_ref, key_ref, value_ref, out_ref, (top_bias_ref, bottom_bias_ref))
    loads[5].wait()


def later_kernel(cols, seg_ref, query_ref, key_ref, value_ref, out_ref, top_bias_ref, bottom_bias_ref):
    fill_biases(seg_ref, (top_bias_ref, bottom_bias_ref))
    query_ref = query_ref.at[:, cols]
    attend_heads(query_ref, key_ref, value_ref, out_ref, (top_bias_ref, bottom_bias_ref))


def near_kernel(seg_ref, query_ref, key_ref, value_ref, out_ref, top_bias_ref, bottom_bias_ref):
    bias_refs = (top_bias_ref, bottom_bias_ref)
    fill_biases(seg_ref, bias_refs)
    attend_heads(query_ref, key_ref, value_ref, out_ref, bias_refs, rolled=True)


def params():
    return pltpu.CompilerParams(vmem_limit_bytes=16 * 1024 * 1024)


def cost(rows, width):
    return pl.CostEstimate(
        flops=4 * rows * rows * width,
        bytes_accessed=4 * rows * width,
        transcendentals=rows * rows * width // HEAD_SIZE,
    )


def biases(tokens):
    half = tokens // 2
    return [pltpu.VMEM((half, half), jnp.float32), pltpu.VMEM((half, tokens), jnp.float32)]


def attend_first(partner, seg_row, queries, keys, values, width):
    tokens = queries.shape[0]
    hbm = pl.BlockSpec(memory_space=pltpu.HBM)
    vmem = pl.BlockSpec(memory_space=pltpu.VMEM)
    operands = (partner, seg_row, queries, keys, values)
    return pl.pallas_call(
        first_kernel,
        out_shape=(
            pltpu.SMEM((1,), jnp.int32),
            pltpu.VMEM(seg_row.shape, jnp.int32),
            pltpu.VMEM((tokens, HEAD_SIZE), jnp.bfloat16),
            pltpu.VMEM((tokens, HEAD_SIZE), jnp.bfloat16),
            pltpu.VMEM((tokens, queries.shape[1] // 2 - width), jnp.bfloat16),
            jax.ShapeDtypeStruct((tokens, width), jnp.bfloat16),
        ),
        in_specs=[hbm] * 5,
        out_specs=(pl.BlockSpec(memory_space=pltpu.SMEM),) + (vmem,) * 5,
        scratch_shapes=[
            pltpu.SMEM(partner.shape, jnp.int32),
            pltpu.VMEM((tokens, width), jnp.bfloat16),
        ]
        + biases(tokens)
        + [pltpu.SemaphoreType.DMA((6,))],
        cost_estimate=cost(tokens, width),
        compiler_params=params(),
    )(*(pltpu.with_memory_space_constraint(operand, pltpu.HBM) for operand in operands))


def attend_later(seg_row, later, key, value, start, width):
    tokens = later.shape[0]
    vmem = pl.BlockSpec(memory_space=pltpu.VMEM)
    return pl.pallas_call(
        functools.partial(later_kernel, slice(start, start + width)),
        out_shape=jax.ShapeDtypeStruct((tokens, width), jnp.bfloat16),
        in_specs=[vmem] * 4,
        out_specs=vmem,
        scratch_shapes=biases(tokens),
        cost_estimate=cost(tokens, width),
        compiler_params=params(),
    )(seg_row, later, key, value)


def attend_near(seg_row, queries, keys, values, kv_head=0):
    tokens = queries.shape[0]
    width = queries.shape[1] // 2
    return pl.pallas_call(
        near_kernel,
        grid=(1,),
        out_shape=jax.ShapeDtypeStruct((tokens, width), jnp.bfloat16),
        in_specs=[
            pl.BlockSpec((1, tokens), lambda i: (0, 0)),
            pl.BlockSpec((tokens, width), lambda i: (0, kv_head)),
            pl.BlockSpec((tokens, HEAD_SIZE), lambda i: (0, kv_head)),
            pl.BlockSpec((tokens, HEAD_SIZE), lambda i: (0, kv_head)),
        ],
        out_specs=pl.BlockSpec((tokens, width), lambda i: (0, 0)),
        scratch_shapes=biases(tokens),
        cost_estimate=cost(tokens, width),
        compiler_params=params(),
    )(seg_row, *(pltpu.with_memory_space_constraint(one, pltpu.HBM) for one in (queries, keys, values)))


def place_kernel(first, part_ref, *refs):
    out_ref, sem = refs[-2:]
    copy = pltpu.make_async_copy(part_ref, out_ref.at[:, pl.ds(first, part_ref.shape[1])], sem)
    copy.start()
    copy.wait()


def place(part, first, width, whole=None):
    operands = (part,) if whole is None else (part, whole)
    return pl.pallas_call(
        functools.partial(place_kernel, first),
        out_shape=pltpu.HBM((part.shape[0], width), part.dtype),
        in_specs=[pl.BlockSpec(memory_space=pl.ANY), pl.BlockSpec(memory_space=pltpu.HBM)][: len(operands)],
        out_specs=pl.BlockSpec(memory_space=pltpu.HBM),
        scratch_shapes=[pltpu.SemaphoreType.DMA],
        input_output_aliases={} if whole is None else {1: 0},
        cost_estimate=pl.CostEstimate(flops=10**10, bytes_accessed=2**28, transcendentals=0),
        compiler_params=params(),
    )(*operands)


def per_device(queries, keys, values, segments, partner):
    tokens = queries.shape[0]
    width = queries.shape[1] // 2
    ranks = lax.axis_size("dp")
    seg_row = segments.reshape(1, tokens)
    if ranks > MOST_SWITCHED:
        second = attend_near(seg_row, queries, keys, values, 1)
        slots = second.reshape(ranks, 1, second.size // ranks)
        spread = lax.all_to_all(slots, "dp", split_axis=0, concat_axis=0, tiled=True)
        onward = jnp.take(spread, partner, axis=0)
        arrived = lax.all_to_all(onward, "dp", split_axis=0, concat_axis=0, tiled=True)
        near = attend_near(seg_row, queries, keys, values)
        return near, arrived.reshape(second.shape)

    widths = [heads * HEAD_SIZE for heads in HEAD_PARTS]
    choice, seg_row, key, value, later, first = attend_first(
        partner, seg_row, queries, keys, values, widths[0]
    )

    def swap(distance):
        pairs = [(rank, rank ^ distance) for rank in range(ranks)]

        def branch(first, later, key, value, seg_row, queries, keys, values):
            arrived = [lax.ppermute(first, "dp", pairs)]
            start = 0
            for part in widths[1:]:
                heads = attend_later(seg_row, later, key, value, start, part)
                arrived.append(lax.ppermute(heads, "dp", pairs))
                start += part
            near = attend_near(seg_row, queries, keys, values)
            lent, start = None, 0
            for heads, part in zip(arrived, widths):
                lent = place(heads, start, width, lent)
                start += part
            return near, lent

        return branch

    branches = [swap(distance) for distance in range(1, ranks)]
    return lax.switch(choice[0], branches, first, later, key, value, seg_row, queries, keys, values)


def solution(mesh):
    rows = P(("groups", "dp"), "tensor")
    return jax.shard_map(
        per_device,
        mesh=mesh,
        in_specs=(rows, rows, rows, P(("groups", "dp")), P("groups")),
        out_specs=(rows, rows),
        check_vma=False,
    )
```
